32 devices in a mesh: group: 4 (over y, x), member: 8 (over z, core).
Axes of the slice: x: 2, y: 2, z: 4, core: 2. Of those that a mesh axis runs over, the one named last changes fastest.
Arguments:
- queries: float32 [256, 768], P(('group', 'member')), may hold values from -6 to 6
- centroids: float32 [1024, 768], P(('group', 'member')), may hold values from -0.21875 to 0.21875
- stored: float32 [16, 2048, 768], P('group', 'member'), may hold values from -0.21875 to 0.21875
- vector_ids: int32 [16, 2048], P('group', 'member'), may hold values from -1 to 32767, as said below
- list_home: int32 [16], replicated, may hold values from 0 to 15, as said below
- probes: int32 [4, 3, 4], replicated, may hold values from 0 to 15, as said below
Outputs:
- coarse_best: float32 [256], P(('group', 'member'))
- fine_best: float32 [3, 256], P(None, ('group', 'member'))
The draws below stay inside these ranges and needn't reach their ends.
Inputs may be any that keep to these rules, and one draw needn't show every extreme that they name: A permutation: list l is stored at slot list_home[l], and slot t belongs to group t // 4. `probes`: for each block and step the 4 probed lists are stored in 4 different groups, one in each. `vector_ids`: ids are distinct where not -1; each list has its valid vectors first, 256 or more of them.
All inputs are finite; a program needn't handle non-finite values.
Results may differ from the reference program's by a relative error of at most 0.0003.
Values sent between devices are 32-bit elements; how exact they have to be, the bound alone decides.
No kernel may reach another device: no remote copies, remote signals or barrier semaphores. Data moves between devices by JAX's collectives and lax.ppermute only.
A program may use at most 64 MiB of HBM per device.

```python
import jax
import jax.numpy as jnp
from jax import lax

D = 768
LG = 4
LEN = 2048
STEPS = 3
GROUPS = 4
BLOCK = 64
QUERIES = 256
CENTROIDS = 1024
LISTS = 16


def probe_tables(key):
    home_slot = jax.random.permutation(jax.random.fold_in(key, 11), LISTS).astype(jnp.int32)
    at_slot = jnp.argsort(home_slot, stable=True).astype(jnp.int32)
    draw_one = jax.random.randint(jax.random.fold_in(key, 12), (GROUPS, STEPS, GROUPS), 0, LG)
    draw_two = jax.random.randint(jax.random.fold_in(key, 13), (GROUPS, STEPS, GROUPS), 0, LG)
    local_pick = jnp.minimum(draw_one, draw_two).astype(jnp.int32)
    owner_rank = jnp.arange(GROUPS, dtype=jnp.int32)[None, None, :]
    chosen = at_slot[owner_rank * LG + local_pick]
    row_keys = jax.random.split(jax.random.fold_in(key, 14), GROUPS * STEPS)
    orders = jax.vmap(lambda kk: jax.random.permutation(kk, GROUPS))(row_keys).reshape(GROUPS, STEPS, GROUPS)
    probe_ids = jnp.take_along_axis(chosen, orders.astype(jnp.int32), axis=2)
    return (home_slot, probe_ids.astype(jnp.int32))


def draw_list_home(key, part):
    home_slot, probe_ids = probe_tables(key)
    return home_slot


def draw_probes(key, part):
    home_slot, probe_ids = probe_tables(key)
    return probe_ids


def draw_vector_ids(key, part):
    shuffled = jax.random.permutation(jax.random.fold_in(key, 21), LISTS * LEN).astype(jnp.int32).reshape(LISTS, LEN)
    lengths = jax.random.randint(jax.random.fold_in(key, 22), (LISTS, 1), LEN // 8, LEN + 1)
    places = jnp.arange(LEN, dtype=jnp.int32)[None, :]
    return jnp.where(places < lengths, shuffled, -1).astype(jnp.int32)


def steps_of(rng, dims, shards, smallest, high):
    def one(position, blocks):
        heights = jax.random.uniform(jax.random.fold_in(jax.random.fold_in(rng, 6), position), (blocks,), jnp.float32, smallest / len(shards), high / len(shards))
        return jnp.repeat(jnp.exp(heights), dims[position] // blocks).reshape((-1,) + (1,) * (len(dims) - position - 1))

    loudness = one(*shards[0])
    for cut in shards[1:]:
        loudness = loudness * one(*cut)
    return loudness


def centred(stream_key, shape, deviation, limit, shards=(), kind=jnp.bfloat16):
    values = deviation * jax.random.normal(stream_key, shape, jnp.float32)
    if shards:
        values = values * steps_of(stream_key, shape, shards, -0.22, 0.18)
    return jnp.clip(values, -limit, limit).astype(kind)


def setup_inputs(seed: int = 0) -> dict:
    streams_of = jax.random.split(jax.random.key(seed), 7)
    queries = centred(streams_of[0], (QUERIES, D), 1.0, 6.0, ((0, 32),), jnp.float32)
    centroids = centred(streams_of[1], (CENTROIDS, D), D ** -0.5, 0.21875, ((0, 32),), jnp.float32)
    stored = centred(streams_of[2], (LISTS, LEN, D), D ** -0.5, 0.21875, ((0, 4), (1, 8)), jnp.float32)
    vector_ids = draw_vector_ids(jax.random.fold_in(streams_of[6], 71), 0)
    list_home = draw_list_home(jax.random.fold_in(streams_of[6], 71), 0)
    probes = draw_probes(jax.random.fold_in(streams_of[6], 71), 0)
    return dict(queries=queries, centroids=centroids, stored=stored, vector_ids=vector_ids, list_home=list_home, probes=probes)


def reference(queries, centroids, stored, vector_ids, list_home, probes):
    blocks = queries.reshape(GROUPS, BLOCK, D)

    def coarse_block(query_block):
        scores = jnp.einsum("qd,cd->qc", query_block, centroids, preferred_element_type=jnp.float32, precision=lax.Precision.HIGHEST)
        return jnp.max(scores, axis=1)

    coarse_best = lax.map(coarse_block, blocks).reshape(-1)

    def fine_group(pair_args):
        query_block, probe_rows = pair_args

        def one_step(list_row):
            slot_ids = list_home[list_row].astype(jnp.int32)
            vectors = stored[slot_ids].reshape(-1, D)
            usable = (vector_ids[slot_ids] >= 0).reshape(-1)
            scores = jnp.einsum("qd,rd->qr", query_block, vectors, preferred_element_type=jnp.float32, precision=lax.Precision.HIGHEST)
            scores = jnp.where(usable[None, :], scores, jnp.float32(-1e30))
            return jnp.max(scores, axis=1)

        return lax.map(one_step, probe_rows)

    fine_all = lax.map(fine_group, (blocks, probes))
    fine_best = jnp.transpose(fine_all, (1, 0, 2)).reshape(STEPS, -1)
    return coarse_best, fine_best
```

```python
import functools

import jax
import jax.numpy as jnp
from jax import lax
from jax.experimental import pallas as pl
from jax.experimental.pallas import tpu as pltpu
from jax.sharding import PartitionSpec as P

LOWEST = -1e30
TILE = 256
NT = (((1,), (1,)), ((), ()))
VMEM_LIMIT = 48 * 2**20


def swapped(value, axis, mask):
    count = lax.axis_size(axis)
    return lax.ppermute(value, axis, [(source, source ^ mask) for source in range(count)])


def gathered(value, axis, first):
    count = lax.axis_size(axis)
    while first < count:
        radix = min(4, count // first)
        arrived = [swapped(value, axis, first * digit) for digit in range(1, radix)]
        value = jnp.concatenate([value, *arrived], axis=0)
        first *= radix
    return value


def split(value):
    high = value.astype(jnp.bfloat16)
    low = (value - high.astype(jnp.float32)).astype(jnp.bfloat16)
    return high, low


def prepare_kernel(block, home_ref, probes_ref, ids_ref, centroids_ref, stored_ref, centers_ref, vectors_ref, places_ref, counts_ref):
    lists, length, depth = stored_ref.shape
    group = lax.axis_index("group")
    for slot in range(lists):
        vectors_ref[slot, :, :depth], vectors_ref[slot, :, depth:] = split(stored_ref[slot])
    centers_ref[:, :depth], centers_ref[:, depth:] = split(centroids_ref[...])
    valid = jnp.sum((ids_ref[...] >= 0).astype(jnp.float32), axis=1, keepdims=True)
    counts_ref[...] = jnp.broadcast_to(valid, counts_ref.shape).astype(jnp.int32)
    blocks, steps, probed = probes_ref.shape
    lane_block = lax.broadcasted_iota(jnp.int32, (1, places_ref.shape[1]), 1) // block
    for step in range(steps):

        def of_block(b, row, step=step):
            place = jnp.int32(-1)
            for j in range(probed):
                slot = home_ref[probes_ref[b, step, j]]
                place = jnp.where(slot // lists == group, slot % lists, place)
            return jnp.where(lane_block == b, place, row)

        row = jnp.full(lane_block.shape, -1, jnp.int32)
        places_ref[pl.ds(step, 1), :] = lax.fori_loop(0, blocks, of_block, row)


def prepare(queries_all, list_home, probes, vector_ids, centroids, stored):
    lists, length, depth = stored.shape
    rows = lists * length + centroids.shape[0]
    smem = pl.BlockSpec(memory_space=pltpu.SMEM)
    vmem = pl.BlockSpec(memory_space=pltpu.VMEM)
    return pl.pallas_call(
        functools.partial(prepare_kernel, queries_all // probes.shape[0]),
        out_shape=(
            jax.ShapeDtypeStruct((centroids.shape[0], 2 * depth), jnp.bfloat16),
            jax.ShapeDtypeStruct((lists, length, 2 * depth), jnp.bfloat16),
            jax.ShapeDtypeStruct((probes.shape[1], queries_all), jnp.int32),
            jax.ShapeDtypeStruct((lists, 128), jnp.int32),
        ),
        in_specs=[smem, smem, vmem, vmem, vmem],
        out_specs=(vmem, vmem, vmem, vmem),
        compiler_params=pltpu.CompilerParams(vmem_limit_bytes=VMEM_LIMIT),
        cost_estimate=pl.CostEstimate(flops=6 * rows * depth, bytes_accessed=8 * rows * depth, transcendentals=0),
        name="prepare",
    )(list_home, probes, vector_ids, centroids, stored)


def score_kernel(rows_dev, own_ref, other_ref, centers_ref, vectors_ref, places_ref, counts_ref, best_ref, queries_ref, parts_ref):
    lists, length, twice = vectors_ref.shape
    depth = twice // 2
    here = lax.axis_index("group") * lax.axis_size("member") + lax.axis_index("member")
    odd = here % 2 == 1
    pairs = TILE // (2 * rows_dev)
    first = pl.program_id(0) * pairs
    for pair in range(pairs):
        start = ((first + pair) ^ (here // 2)) * rows_dev
        source = pl.ds(pl.multiple_of(start, rows_dev), rows_dev)
        own, other = own_ref[source, :], other_ref[source, :]
        at = 2 * pair * rows_dev
        queries_ref[pl.ds(at, rows_dev), :] = jnp.where(odd, other, own)
        queries_ref[pl.ds(at + rows_dev, rows_dev), :] = jnp.where(odd, own, other)
    high, low = split(queries_ref[...])
    parts_ref[:, :depth] = high
    parts_ref[:, depth:twice] = high
    parts_ref[:, twice:] = low

    def scores(vectors):
        return lax.dot_general(vectors[...], parts_ref[:, :twice], NT, preferred_element_type=jnp.float32) + lax.dot_general(
            vectors[:, :depth], parts_ref[:, twice:], NT, preferred_element_type=jnp.float32
        )

    fine = [jnp.full((1, TILE), LOWEST, jnp.float32) for _ in range(places_ref.shape[0])]
    place = lax.broadcasted_iota(jnp.int32, (length, TILE), 0)
    for slot in range(lists):
        count = jnp.concatenate([counts_ref[pl.ds(slot, 1), :]] * (TILE // 128), axis=1)
        usable = jnp.where(place < count, scores(vectors_ref.at[slot]), LOWEST)
        best = jnp.max(usable, axis=0, keepdims=True)
        for step in range(len(fine)):
            fine[step] = jnp.where(places_ref[pl.ds(step, 1), :] == slot, best, fine[step])
    coarse = jnp.max(scores(centers_ref), axis=0, keepdims=True)
    best_ref[...] = jnp.concatenate([coarse, *fine], axis=0)


def score(rows_dev, own, other, centers, vectors, places, counts):
    queries_all, depth = 2 * own.shape[0], own.shape[1]
    whole = pl.BlockSpec(memory_space=pltpu.VMEM)
    rows = vectors.shape[0] * vectors.shape[1] + centers.shape[0]
    steps = places.shape[0]
    return pl.pallas_call(
        functools.partial(score_kernel, rows_dev),
        out_shape=jax.ShapeDtypeStruct((1 + steps, queries_all), jnp.float32),
        grid=(queries_all // TILE,),
        in_specs=[whole, whole, whole, whole, pl.BlockSpec((steps, TILE), lambda i: (0, i)), whole],
        out_specs=pl.BlockSpec((1 + steps, TILE), lambda i: (0, i)),
        scratch_shapes=[pltpu.VMEM((TILE, depth), jnp.float32), pltpu.VMEM((TILE, 3 * depth), jnp.bfloat16)],
        compiler_params=pltpu.CompilerParams(vmem_limit_bytes=VMEM_LIMIT),
        cost_estimate=pl.CostEstimate(flops=6 * rows * queries_all * depth, bytes_accessed=4 * rows * depth, transcendentals=0),
        name="score",
    )(own, other, centers, vectors, places, counts)


def local(queries, centroids, stored, vector_ids, list_home, probes):
    devices = lax.axis_size("group") * lax.axis_size("member")
    rows_dev = queries.shape[0]
    ready = prepare(devices * rows_dev, list_home, probes, vector_ids, centroids, stored)
    own = gathered(gathered(queries, "member", 2), "group", 1)
    other = swapped(own, "member", 1)
    best = score(rows_dev, own, other, *ready)
    kinds = best.shape[0]
    parts = best.reshape(kinds, devices, rows_dev).transpose(1, 0, 2)
    final = jnp.max(lax.all_to_all(parts, ("group", "member"), 0, 0, tiled=True), axis=0)
    return final[0], final[1:]


def solution(mesh):
    placed = (
        P(("group", "member"), None),
        P(("group", "member"), None),
        P("group", "member", None),
        P("group", "member"),
        P(),
        P(),
    )
    return jax.shard_map(
        local,
        mesh=mesh,
        in_specs=placed,
        out_specs=(P(("group", "member")), P(None, ("group", "member"))),
        check_vma=False,
    )
```

```python
import functools

import jax
import jax.numpy as jnp
from jax import lax
from jax.experimental import pallas as pl
from jax.experimental.pallas import tpu as pltpu
from jax.sharding import PartitionSpec as P

LOWEST = -1e30
TILE = 128
BOTH = ("group", "member")
NT = (((1,), (1,)), ((), ()))
LARGE = 48 * 2**20
SMALL = 16 * 2**20
WHOLE = pl.BlockSpec(memory_space=pltpu.VMEM)
ANYWHERE = pl.BlockSpec(memory_space=pl.ANY)


def stages():
    members, groups = lax.axis_size("member"), lax.axis_size("group")
    inner = [1 << k for k in range(1, members.bit_length() - 1)]
    outer = [members << k for k in range(groups.bit_length() - 1)]
    listed = []
    for bits in (inner, outer):
        for at in range(0, len(bits), 2):
            low, *rest = bits[at : at + 2]
            listed.append([low | rest[0], rest[0], low] if rest else [low])
    return listed


def exchanged(value, mask):
    devices = lax.axis_size("group") * lax.axis_size("member")
    return lax.ppermute(value, BOTH, [(d, d ^ mask) for d in range(devices)])


def positions():
    offsets = [0]
    for stage in stages():
        offsets = [offset ^ mask for mask in [0, *stage] for offset in offsets]
    return [offsets.index(2 << k) for k in range(len(offsets).bit_length() - 1)]


def position(chip):
    place = 0
    for k, at in enumerate(positions()):
        place = place ^ (((chip >> k) & 1) * at)
    return place


def here():
    return lax.axis_index("group") * lax.axis_size("member") + lax.axis_index("member")


def crossed(chips):
    found = 0
    for stage in stages():
        mask = functools.reduce(lambda a, b: a | b, stage) >> 1
        found = found ^ jnp.where((chips & mask) != 0, 1, 0)
    return found


def split(value):
    high = value.astype(jnp.bfloat16)
    low = (value - high.astype(jnp.float32)).astype(jnp.bfloat16)
    return high, low


def lookup_kernel(home_hbm, probes_hbm, ids_hbm, places_ref, counts_ref, home_ref, probes_ref, ids_ref, sems, *, lists, lanes):
    copies = [
        pltpu.make_async_copy(source, target, sems.at[k])
        for k, (source, target) in enumerate([(home_hbm, home_ref), (probes_hbm, probes_ref), (ids_hbm, ids_ref)])
    ]
    for copy in copies:
        copy.start()
    for copy in copies:
        copy.wait()
    group = lax.axis_index("group")
    valid = jnp.sum((ids_ref[...] >= 0).astype(jnp.float32), axis=1, keepdims=True)
    counts_ref[...] = jnp.broadcast_to(valid, counts_ref.shape).astype(jnp.int32)
    steps, blocks, probed = probes_ref.shape
    lane_block = lax.broadcasted_iota(jnp.int32, (1, places_ref.shape[1]), 1) // lanes
    for step in range(steps):

        def of_block(b, row, step=step):
            place = jnp.int32(-1)
            for j in range(probed):
                slot = home_ref[probes_ref[step, b, j]]
                place = jnp.where(slot // lists == group, slot % lists, place)
            return jnp.where(lane_block == b, place, row)

        row = jnp.full(lane_block.shape, -1, jnp.int32)
        places_ref[pl.ds(step, 1), :] = lax.fori_loop(0, blocks, of_block, row)


def lookup(half, list_home, probes, vector_ids):
    steps, blocks, _ = probes.shape
    lists = vector_ids.shape[0]
    return pl.pallas_call(
        functools.partial(lookup_kernel, lists=lists, lanes=half // blocks),
        out_shape=(
            jax.ShapeDtypeStruct((steps, half), jnp.int32),
            jax.ShapeDtypeStruct((lists, TILE), jnp.int32),
        ),
        in_specs=[ANYWHERE] * 3,
        out_specs=(WHOLE, WHOLE),
        scratch_shapes=[
            pltpu.SMEM(list_home.shape, jnp.int32),
            pltpu.SMEM(probes.shape, jnp.int32),
            pltpu.VMEM(vector_ids.shape, jnp.int32),
            pltpu.SemaphoreType.DMA((3,)),
        ],
        compiler_params=pltpu.CompilerParams(vmem_limit_bytes=SMALL),
        cost_estimate=pl.CostEstimate(flops=10000, bytes_accessed=100000, transcendentals=0),
        name="lookup",
    )(list_home, probes, vector_ids)


def prepare_kernel(centroids_hbm, stored_hbm, centers_ref, vectors_ref, centroids_ref, stored_ref, sems):
    lists, length, _ = stored_ref.shape
    count = centroids_ref.shape[0]
    copies = [pltpu.make_async_copy(stored_hbm.at[k], stored_ref.at[k], sems.at[k]) for k in range(lists)]
    copies.append(pltpu.make_async_copy(centroids_hbm, centroids_ref, sems.at[lists]))
    for copy in copies:
        copy.start()
    for k in range(lists):
        copies[k].wait()
        vectors_ref[k, :length], vectors_ref[k, length:] = split(stored_ref[k])
    copies[lists].wait()
    centers_ref[:count], centers_ref[count:] = split(centroids_ref[...])


def prepare(centroids, stored):
    lists, length, depth = stored.shape
    rows = lists * length + centroids.shape[0]
    return pl.pallas_call(
        prepare_kernel,
        out_shape=(
            jax.ShapeDtypeStruct((2 * centroids.shape[0], depth), jnp.bfloat16),
            jax.ShapeDtypeStruct((lists, 2 * length, depth), jnp.bfloat16),
        ),
        in_specs=[ANYWHERE] * 2,
        out_specs=(WHOLE, WHOLE),
        scratch_shapes=[
            pltpu.VMEM(centroids.shape, jnp.float32),
            pltpu.VMEM(stored.shape, jnp.float32),
            pltpu.SemaphoreType.DMA((lists + 1,)),
        ],
        compiler_params=pltpu.CompilerParams(vmem_limit_bytes=LARGE),
        cost_estimate=pl.CostEstimate(flops=6 * rows * depth, bytes_accessed=8 * rows * depth, transcendentals=0),
        name="prepare",
    )(centroids, stored)


def best_scores(rows_dev, blocks_ref, centers_ref, vectors_ref, places_ref, counts_ref, queries_ref, parts_ref):
    lists, length = vectors_ref.shape[0], vectors_ref.shape[1] // 2
    origin = position(here() >> 1)
    chunks = TILE // rows_dev
    for chunk in range(chunks):
        offset = position(chunk if blocks_ref.shape[0] == TILE else pl.program_id(0) * chunks + chunk)
        source = pl.multiple_of((origin ^ offset) * rows_dev, rows_dev)
        queries_ref[pl.ds(chunk * rows_dev, rows_dev), :] = blocks_ref[pl.ds(source, rows_dev), :]
    parts_ref[:TILE], parts_ref[TILE:] = split(queries_ref[...])

    def scores(vectors):
        count = vectors.shape[0] // 2
        terms = lax.dot_general(vectors[...], parts_ref[...], NT, preferred_element_type=jnp.float32)
        small = terms[:count, TILE:] + (terms[count:, :TILE] + terms[count:, TILE:])
        return terms[:count, :TILE] + small

    fine = [jnp.full((1, TILE), LOWEST, jnp.float32) for _ in range(places_ref.shape[0])]
    place = lax.broadcasted_iota(jnp.int32, (length, TILE), 0)
    for slot in range(lists):
        usable = jnp.where(place < counts_ref[pl.ds(slot, 1), :], scores(vectors_ref.at[slot]), LOWEST)
        best = jnp.max(usable, axis=0, keepdims=True)
        for step in range(len(fine)):
            fine[step] = jnp.where(places_ref[pl.ds(step, 1), :] == slot, best, fine[step])
    coarse = jnp.max(scores(centers_ref), axis=0, keepdims=True)
    return jnp.concatenate([coarse, *fine], axis=0)


def own_kernel(*refs, rows_dev):
    *ins, best_ref, queries_ref, parts_ref = refs
    best_ref[0] = best_scores(rows_dev, *ins, queries_ref, parts_ref)


def other_kernel(own_ref, *refs, rows_dev):
    *ins, out_ref, queries_ref, parts_ref = refs
    own, other = own_ref[0], best_scores(rows_dev, *ins, queries_ref, parts_ref)
    chips = out_ref.shape[0] // 2
    for chip in range(chips):
        straight = crossed((pl.program_id(0) * chips + chip) ^ (here() >> 1)) == (here() & 1)
        out_ref[2 * chip] = jnp.where(straight, own, other)
        out_ref[2 * chip + 1] = jnp.where(straight, other, own)


def score(rows_dev, kernel, blocks, centers, vectors, places, counts, own=None):
    half, depth = blocks.shape
    rows = vectors.shape[0] * vectors.shape[1] // 2 + centers.shape[0] // 2
    kinds = 1 + places.shape[0]
    per = pl.BlockSpec((1, kinds, TILE), lambda i: (i, 0, 0))
    devices = 2 * TILE // rows_dev
    return pl.pallas_call(
        functools.partial(kernel, rows_dev=rows_dev),
        out_shape=jax.ShapeDtypeStruct((half // TILE * (1 if own is None else devices), kinds, TILE), jnp.float32),
        grid=(half // TILE,),
        in_specs=[*([] if own is None else [per]), WHOLE, WHOLE, WHOLE, pl.BlockSpec((kinds - 1, TILE), lambda i: (0, i)), WHOLE],
        out_specs=per if own is None else pl.BlockSpec((devices, kinds, TILE), lambda i: (i, 0, 0)),
        scratch_shapes=[pltpu.VMEM((TILE, depth), jnp.float32), pltpu.VMEM((2 * TILE, depth), jnp.bfloat16)],
        compiler_params=pltpu.CompilerParams(vmem_limit_bytes=LARGE),
        cost_estimate=pl.CostEstimate(flops=8 * rows * half * depth, bytes_accessed=4 * rows * depth, transcendentals=0),
        name=kernel.__name__,
    )(*([] if own is None else [own]), blocks, centers, vectors, places, counts)


def finish_kernel(arrived_ref, coarse_ref, fine_ref, *, rows_dev):
    best = jnp.max(arrived_ref[...], axis=0)
    lane = ((here() >> 1) * rows_dev) % TILE
    best = pltpu.roll(best, (TILE - lane) % TILE, 1)
    coarse_ref[...] = best[0, :rows_dev]
    fine_ref[...] = best[1:, :rows_dev]


def finish(rows_dev, arrived):
    kinds = arrived.shape[1]
    return pl.pallas_call(
        functools.partial(finish_kernel, rows_dev=rows_dev),
        out_shape=(
            jax.ShapeDtypeStruct((rows_dev,), jnp.float32),
            jax.ShapeDtypeStruct((kinds - 1, rows_dev), jnp.float32),
        ),
        in_specs=[WHOLE],
        out_specs=(WHOLE, WHOLE),
        compiler_params=pltpu.CompilerParams(vmem_limit_bytes=SMALL),
        name="finish",
    )(arrived)


def gathered(blocks, stage):
    return jnp.concatenate([blocks, *[exchanged(blocks, mask | 1) for mask in stage]], axis=0)


def local(queries, centroids, stored, vector_ids, list_home, probes):
    devices = lax.axis_size("group") * lax.axis_size("member")
    rows_dev = queries.shape[0]
    found = lookup(devices // 2 * rows_dev, list_home, probes.transpose(1, 0, 2), vector_ids)
    blocks = queries
    *early, last = stages()
    for stage in early:
        blocks = gathered(blocks, stage)
    blocks, centroids, stored, *found = lax.optimization_barrier((blocks, centroids, stored, *found))
    blocks, *split_vectors = lax.optimization_barrier((gathered(blocks, last), *prepare(centroids, stored)))
    ready = (*split_vectors, *found)
    theirs = exchanged(blocks, 1)
    own = score(rows_dev, own_kernel, blocks, *ready)
    parts = score(rows_dev, other_kernel, theirs, *ready, own=own)
    return finish(rows_dev, lax.all_to_all(parts, BOTH, 0, 0, tiled=True))


def solution(mesh):
    placed = (
        P(BOTH, None),
        P(BOTH, None),
        P("group", "member", None),
        P("group", "member"),
        P(),
        P(),
    )
    return jax.shard_map(
        local,
        mesh=mesh,
        in_specs=placed,
        out_specs=(P(BOTH), P(None, BOTH)),
        check_vma=False,
    )
```

```python
import functools

import jax
import jax.numpy as jnp
from jax import lax
from jax.experimental import pallas as pl
from jax.experimental.pallas import tpu as pltpu
from jax.sharding import PartitionSpec as P

LOWEST = -1e30
TILE = 128
BOTH = ("group", "member")
NT = (((1,), (1,)), ((), ()))
LARGE = 20 * 2**20
SMALL = 10 * 2**20
WHOLE = pl.BlockSpec(memory_space=pltpu.VMEM)
ANYWHERE = pl.BlockSpec(memory_space=pl.ANY)


def stages():
    members, groups = lax.axis_size("member"), lax.axis_size("group")
    inner = [1 << k for k in range(1, members.bit_length() - 1)]
    outer = [members << k for k in range(groups.bit_length() - 1)]
    listed = []
    for bits in (inner, outer):
        for at in range(0, len(bits), 2):
            low, *rest = bits[at : at + 2]
            listed.append([low | rest[0], rest[0], low] if rest else [low])
    return listed


def exchanged(value, mask):
    devices = lax.axis_size("group") * lax.axis_size("member")
    return lax.ppermute(value, BOTH, [(d, d ^ mask) for d in range(devices)])


def positions():
    offsets = [0]
    for stage in stages():
        offsets = [offset ^ mask for mask in [0, *stage] for offset in offsets]
    return [offsets.index(2 << k) for k in range(len(offsets).bit_length() - 1)]


def position(chip):
    place = 0
    for k, at in enumerate(positions()):
        place = place ^ (((chip >> k) & 1) * at)
    return place


def here():
    return lax.axis_index("group") * lax.axis_size("member") + lax.axis_index("member")


def crossed(chips):
    found = 0
    for stage in stages():
        mask = functools.reduce(lambda a, b: a | b, stage) >> 1
        found = found ^ jnp.where((chips & mask) != 0, 1, 0)
    return found


def split(value):
    high = value.astype(jnp.bfloat16)
    low = (value - high.astype(jnp.float32)).astype(jnp.bfloat16)
    return high, low


def copy_all(pairs, sems):
    copies = [pltpu.make_async_copy(source, target, sems.at[k]) for k, (source, target) in enumerate(pairs)]
    for copy in copies:
        copy.start()
    return copies


def lookup_kernel(home_hbm, probes_hbm, ids_hbm, theirs_hbm, places_ref, counts_ref, home_ref, probes_ref, ids_ref, sems, *, lanes):
    lists = ids_ref.shape[1]
    pairs = [(home_hbm, home_ref), (probes_hbm, probes_ref), (ids_hbm, ids_ref.at[0]), (theirs_hbm, ids_ref.at[1])]
    for copy in copy_all(pairs, sems):
        copy.wait()
    group = lax.axis_index("group")
    valid = jnp.sum((ids_ref[...] >= 0).astype(jnp.float32), axis=2, keepdims=True)
    counts_ref[...] = jnp.broadcast_to(valid, counts_ref.shape).astype(jnp.int32)
    steps, blocks, probed = probes_ref.shape
    lane_block = lax.broadcasted_iota(jnp.int32, (1, places_ref.shape[1]), 1) // lanes
    for step in range(steps):

        def of_block(b, row, step=step):
            place = jnp.int32(-1)
            for j in range(probed):
                slot = home_ref[probes_ref[step, b, j]]
                place = jnp.where(slot // lists == group, slot % lists, place)
            return jnp.where(lane_block == b, place, row)

        row = jnp.full(lane_block.shape, -1, jnp.int32)
        places_ref[pl.ds(step, 1), :] = lax.fori_loop(0, blocks, of_block, row)


def lookup(half, list_home, probes, vector_ids, theirs):
    steps, blocks, _ = probes.shape
    lists = vector_ids.shape[0]
    return pl.pallas_call(
        functools.partial(lookup_kernel, lanes=half // blocks),
        out_shape=(
            jax.ShapeDtypeStruct((steps, half), jnp.int32),
            jax.ShapeDtypeStruct((2, lists, TILE), jnp.int32),
        ),
        in_specs=[ANYWHERE] * 4,
        out_specs=(WHOLE, WHOLE),
        scratch_shapes=[
            pltpu.SMEM(list_home.shape, jnp.int32),
            pltpu.SMEM(probes.shape, jnp.int32),
            pltpu.VMEM((2, *vector_ids.shape), jnp.int32),
            pltpu.SemaphoreType.DMA((4,)),
        ],
        compiler_params=pltpu.CompilerParams(vmem_limit_bytes=SMALL),
        cost_estimate=pl.CostEstimate(flops=10000, bytes_accessed=100000, transcendentals=0),
        name="lookup",
    )(list_home, probes, vector_ids, theirs)


def split_kernel(centroids_hbm, stored_hbm, *refs):
    *passed, centroids_ref, stored_ref, sems = refs
    if len(passed) == 4:
        queries_hbm, centers_ref, vectors_ref, queries_ref = passed
        extra = [(queries_hbm, queries_ref)]
    else:
        centers_ref, vectors_ref = passed
        extra = []
    lists, length, _ = stored_ref.shape
    count = centroids_ref.shape[0]
    pairs = [(centroids_hbm, centroids_ref), *extra, *[(stored_hbm.at[k], stored_ref.at[k]) for k in range(lists)]]
    copies = copy_all(pairs, sems)
    for copy in copies[:-lists]:
        copy.wait()
    centers_ref[:count], centers_ref[count:] = split(centroids_ref[...])
    for k in range(lists):
        copies[k - lists].wait()
        vectors_ref[k, :length], vectors_ref[k, length:] = split(stored_ref[k])


def prepare(centroids, stored, *queries):
    lists, length, depth = stored.shape
    rows = lists * length + centroids.shape[0]
    return pl.pallas_call(
        split_kernel,
        out_shape=(
            jax.ShapeDtypeStruct((2 * centroids.shape[0], depth), jnp.bfloat16),
            jax.ShapeDtypeStruct((lists, 2 * length, depth), jnp.bfloat16),
            *[jax.ShapeDtypeStruct(q.shape, q.dtype) for q in queries],
        ),
        in_specs=[ANYWHERE] * (2 + len(queries)),
        out_specs=(WHOLE,) * (2 + len(queries)),
        scratch_shapes=[
            pltpu.VMEM(centroids.shape, jnp.float32),
            pltpu.VMEM(stored.shape, jnp.float32),
            pltpu.SemaphoreType.DMA((lists + 1 + len(queries),)),
        ],
        compiler_params=pltpu.CompilerParams(vmem_limit_bytes=LARGE),
        cost_estimate=pl.CostEstimate(flops=6 * rows * depth, bytes_accessed=8 * rows * depth, transcendentals=0),
        name="prepare",
    )(centroids, stored, *queries)


def score_kernel(blocks_ref, places_ref, counts_ref, *refs, rows_dev):
    *halves, out_ref, queries_ref, parts_ref = refs
    origin = here() >> 1
    chunks = TILE // rows_dev
    first = position(origin)
    for chunk in range(chunks):
        offset = position(chunk if blocks_ref.shape[0] == TILE else pl.program_id(0) * chunks + chunk)
        source = pl.multiple_of((first ^ offset) * rows_dev, rows_dev)
        queries_ref[pl.ds(chunk * rows_dev, rows_dev), :] = blocks_ref[pl.ds(source, rows_dev), :]
    parts_ref[:TILE], parts_ref[TILE:] = split(queries_ref[...])

    def scores(vectors):
        count = vectors.shape[0] // 2
        terms = lax.dot_general(vectors[...], parts_ref[...], NT, preferred_element_type=jnp.float32)
        small = terms[:count, TILE:] + (terms[count:, :TILE] + terms[count:, TILE:])
        return terms[:count, :TILE] + small

    best = [jnp.full((1, TILE), LOWEST, jnp.float32) for _ in range(1 + places_ref.shape[0])]
    for side in range(2):
        centers_ref, vectors_ref = halves[2 * side : 2 * side + 2]
        lists, length = vectors_ref.shape[0], vectors_ref.shape[1] // 2
        place = lax.broadcasted_iota(jnp.int32, (length, TILE), 0)
        best[0] = jnp.maximum(best[0], jnp.max(scores(centers_ref), axis=0, keepdims=True))
        for slot in range(lists):
            usable = jnp.where(place < counts_ref[side, pl.ds(slot, 1), :], scores(vectors_ref.at[slot]), LOWEST)
            found = jnp.max(usable, axis=0, keepdims=True)
            for step in range(places_ref.shape[0]):
                chosen = jnp.where(places_ref[pl.ds(step, 1), :] == slot, found, LOWEST)
                best[1 + step] = jnp.maximum(best[1 + step], chosen)
    best = jnp.concatenate(best, axis=0)
    nothing = jnp.full(best.shape, LOWEST, jnp.float32)
    for chip in range(chunks):
        straight = crossed((pl.program_id(0) * chunks + chip) ^ origin) == (here() & 1)
        out_ref[2 * chip] = jnp.where(straight, best, nothing)
        out_ref[2 * chip + 1] = jnp.where(straight, nothing, best)


def score(rows_dev, blocks, places, counts, *halves):
    half, depth = blocks.shape
    kinds = 1 + places.shape[0]
    rows = halves[0].shape[0] + halves[1].shape[0] * halves[1].shape[1]
    devices = 2 * TILE // rows_dev
    return pl.pallas_call(
        functools.partial(score_kernel, rows_dev=rows_dev),
        out_shape=jax.ShapeDtypeStruct((half // TILE * devices, kinds, TILE), jnp.float32),
        grid=(half // TILE,),
        in_specs=[WHOLE, pl.BlockSpec((kinds - 1, TILE), lambda i: (0, i)), WHOLE, *[WHOLE] * len(halves)],
        out_specs=pl.BlockSpec((devices, kinds, TILE), lambda i: (i, 0, 0)),
        scratch_shapes=[pltpu.VMEM((TILE, depth), jnp.float32), pltpu.VMEM((2 * TILE, depth), jnp.bfloat16)],
        compiler_params=pltpu.CompilerParams(vmem_limit_bytes=LARGE),
        cost_estimate=pl.CostEstimate(flops=8 * rows * half * depth, bytes_accessed=4 * rows * depth, transcendentals=0),
        name="score",
    )(blocks, places, counts, *halves)


def finish_kernel(arrived_ref, coarse_ref, fine_ref, *, rows_dev):
    best = jnp.max(arrived_ref[...], axis=0)
    lane = ((here() >> 1) * rows_dev) % TILE
    best = pltpu.roll(best, (TILE - lane) % TILE, 1)
    coarse_ref[...] = best[0, :rows_dev]
    fine_ref[...] = best[1:, :rows_dev]


def finish(rows_dev, arrived):
    kinds = arrived.shape[1]
    return pl.pallas_call(
        functools.partial(finish_kernel, rows_dev=rows_dev),
        out_shape=(
            jax.ShapeDtypeStruct((rows_dev,), jnp.float32),
            jax.ShapeDtypeStruct((kinds - 1, rows_dev), jnp.float32),
        ),
        in_specs=[WHOLE],
        out_specs=(WHOLE, WHOLE),
        compiler_params=pltpu.CompilerParams(vmem_limit_bytes=SMALL),
        name="finish",
    )(arrived)


def gathered(blocks, stage):
    return [exchanged(blocks, mask | 1) for mask in stage]


def in_hbm(*arrays):
    return [pltpu.with_memory_space_constraint(array, pltpu.HBM) for array in arrays]


def local(queries, centroids, stored, vector_ids, list_home, probes):
    devices = lax.axis_size("group") * lax.axis_size("member")
    rows_dev = queries.shape[0]
    first, *rest = stages()
    arrived = gathered(queries, first)
    theirs = [exchanged(array, 1) for array in (centroids, stored, vector_ids)]
    *own, copied = prepare(*in_hbm(centroids, stored, queries))
    blocks = jnp.concatenate([copied, *arrived], axis=0)
    for number, stage in enumerate(rest):
        blocks, *own = lax.optimization_barrier((blocks, *own))
        arrived = gathered(blocks, stage)
        if number == len(rest) - 1:
            other = prepare(*theirs[:2])
            found = lookup(devices // 2 * rows_dev, *in_hbm(list_home, probes.transpose(1, 0, 2), vector_ids), theirs[2])
            ready = lax.optimization_barrier((*arrived, *found, *own, *other))
            arrived, ready = ready[: len(stage)], ready[len(stage) :]
        blocks = jnp.concatenate([blocks, *arrived], axis=0)
    parts = score(rows_dev, blocks, *ready)
    return finish(rows_dev, lax.all_to_all(parts, BOTH, 0, 0, tiled=True))


def solution(mesh):
    placed = (
        P(BOTH, None),
        P(BOTH, None),
        P("group", "member", None),
        P("group", "member"),
        P(),
        P(),
    )
    return jax.shard_map(
        local,
        mesh=mesh,
        in_specs=placed,
        out_specs=(P(BOTH), P(None, BOTH)),
        check_vma=False,
    )
```

```python
import functools

import jax
import jax.numpy as jnp
from jax import lax
from jax.experimental import pallas as pl
from jax.experimental.pallas import tpu as pltpu
from jax.sharding import PartitionSpec as P

LOWEST = -1e30
TILE = 128
EIGHT = jnp.float8_e4m3fn
SCALE = 2.0**16
BOTH = ("group", "member")
NT = (((1,), (1,)), ((), ()))
LARGE = 20 * 2**20
SMALL = 10 * 2**20
WHOLE = pl.BlockSpec(memory_space=pltpu.VMEM)
ANYWHERE = pl.BlockSpec(memory_space=pl.ANY)


def stages():
    members, groups = lax.axis_size("member"), lax.axis_size("group")
    inner = [1 << k for k in range(1, members.bit_length() - 1)]
    outer = [members << k for k in range(groups.bit_length() - 1)]
    listed = []
    for bits, order in ((inner, (2, 1, 3)), (outer, (3, 2, 1))):
        for at in range(0, len(bits), 2):
            pair = bits[at : at + 2]
            listed.append([pair[0] * value | 1 for value in order[: 2 * len(pair) - 1] if len(pair) == 2] or [pair[0] | 1])
    return listed


def exchanged(value, mask):
    devices = lax.axis_size("group") * lax.axis_size("member")
    return lax.ppermute(value, BOTH, [(d, d ^ mask) for d in range(devices)])


def positions():
    offsets = [0]
    for stage in stages():
        offsets = [offset ^ (mask >> 1) for mask in [0, *stage] for offset in offsets]
    return [offsets.index(1 << k) for k in range(len(offsets).bit_length() - 1)]


def position(chip):
    place = 0
    for k, at in enumerate(positions()):
        place = place ^ (((chip >> k) & 1) * at)
    return place


def here():
    return lax.axis_index("group") * lax.axis_size("member") + lax.axis_index("member")


def crossed(chips):
    found = 0
    for stage in stages():
        bits = functools.reduce(lambda a, b: a | b, stage) >> 1
        for mask in stage:
            if mask & 1:
                found = found ^ jnp.where((chips & bits) == mask >> 1, 1, 0)
    return found


def split(value):
    high = value.astype(jnp.bfloat16)
    return high, value - high.astype(jnp.float32)


def copy_all(pairs, sems):
    copies = [pltpu.make_async_copy(source, target, sems.at[k]) for k, (source, target) in enumerate(pairs)]
    for copy in copies:
        copy.start()
    return copies


def lookup_kernel(home_hbm, probes_hbm, queries_hbm, places_ref, queries_ref, home_ref, probes_ref, sems, *, lists, lanes):
    copies = copy_all([(home_hbm, home_ref), (probes_hbm, probes_ref), (queries_hbm, queries_ref)], sems)
    copies[0].wait()
    copies[1].wait()
    group = lax.axis_index("group")
    steps, blocks, probed = probes_ref.shape
    lane_block = lax.broadcasted_iota(jnp.int32, (1, places_ref.shape[1]), 1) // lanes
    for step in range(steps):

        def of_block(b, row, step=step):
            place = jnp.int32(-1)
            for j in range(probed):
                slot = home_ref[probes_ref[step, b, j]]
                place = jnp.where(slot // lists == group, slot % lists, place)
            return jnp.where(lane_block == b, place, row)

        row = jnp.full(lane_block.shape, -1, jnp.int32)
        places_ref[pl.ds(step, 1), :] = lax.fori_loop(0, blocks, of_block, row)
    copies[2].wait()


def lookup(half, lists, list_home, probes, queries):
    steps, blocks, _ = probes.shape
    return pl.pallas_call(
        functools.partial(lookup_kernel, lists=lists, lanes=half // blocks),
        out_shape=(
            jax.ShapeDtypeStruct((steps, half), jnp.int32),
            jax.ShapeDtypeStruct(queries.shape, queries.dtype),
        ),
        in_specs=[ANYWHERE] * 3,
        out_specs=(WHOLE, WHOLE),
        scratch_shapes=[
            pltpu.SMEM(list_home.shape, jnp.int32),
            pltpu.SMEM(probes.shape, jnp.int32),
            pltpu.SemaphoreType.DMA((3,)),
        ],
        compiler_params=pltpu.CompilerParams(vmem_limit_bytes=SMALL),
        cost_estimate=pl.CostEstimate(flops=10000, bytes_accessed=100000, transcendentals=0),
        name="lookup",
    )(list_home, probes, queries)


def split_vectors(value):
    high, low = split(value)
    return high, (low * SCALE).astype(EIGHT)


def split_lists(centroids_ref, ids_ref, stored_ref, *refs, arrived=lambda k: None):
    centers_ref, centers_low_ref, counts_ref, vectors_ref, vectors_low_ref = refs
    arrived(0)
    arrived(1)
    centers_ref[...], centers_low_ref[...] = split_vectors(centroids_ref[...])
    valid = jnp.sum((ids_ref[...] >= 0).astype(jnp.float32), axis=1, keepdims=True)
    counts_ref[...] = jnp.broadcast_to(valid, counts_ref.shape).astype(jnp.int32)
    for k in range(stored_ref.shape[0]):
        arrived(2 + k)
        vectors_ref[k], vectors_low_ref[k] = split_vectors(stored_ref[k])


def copied_kernel(centroids_hbm, ids_hbm, stored_hbm, *refs):
    *outs, centroids_ref, ids_ref, stored_ref, sems = refs
    lists = stored_ref.shape[0]
    pairs = [(centroids_hbm, centroids_ref), (ids_hbm, ids_ref), *[(stored_hbm.at[k], stored_ref.at[k]) for k in range(lists)]]
    copies = copy_all(pairs, sems)
    split_lists(centroids_ref, ids_ref, stored_ref, *outs, arrived=lambda k: copies[k].wait())


def prepare(centroids, ids, stored, copied):
    lists, length, depth = stored.shape
    rows = lists * length + centroids.shape[0]
    scratch = [pltpu.VMEM(array.shape, array.dtype) for array in (centroids, ids, stored)]
    return pl.pallas_call(
        copied_kernel if copied else split_lists,
        out_shape=(
            jax.ShapeDtypeStruct(centroids.shape, jnp.bfloat16),
            jax.ShapeDtypeStruct(centroids.shape, EIGHT),
            jax.ShapeDtypeStruct((lists, TILE), jnp.int32),
            jax.ShapeDtypeStruct(stored.shape, jnp.bfloat16),
            jax.ShapeDtypeStruct(stored.shape, EIGHT),
        ),
        in_specs=[ANYWHERE if copied else WHOLE] * 3,
        out_specs=(WHOLE,) * 5,
        scratch_shapes=[*scratch, pltpu.SemaphoreType.DMA((2 + lists,))] if copied else [],
        compiler_params=pltpu.CompilerParams(vmem_limit_bytes=SMALL),
        cost_estimate=pl.CostEstimate(flops=6 * rows * depth, bytes_accessed=8 * rows * depth, transcendentals=0),
        name="prepare",
    )(centroids, ids, stored)


def score_kernel(blocks_ref, places_ref, *refs, rows_dev):
    *halves, out_ref, queries_ref, parts_ref, eighth_ref = refs
    origin = here() >> 1
    chunks = TILE // rows_dev
    first = position(origin)
    for chunk in range(chunks):
        offset = position(chunk if blocks_ref.shape[0] == TILE else pl.program_id(0) * chunks + chunk)
        source = pl.multiple_of((first ^ offset) * rows_dev, rows_dev)
        queries_ref[pl.ds(chunk * rows_dev, rows_dev), :] = blocks_ref[pl.ds(source, rows_dev), :]
    high, low = split(queries_ref[...])
    parts_ref[:TILE], parts_ref[TILE:] = high, low.astype(jnp.bfloat16)
    eighth_ref[...] = queries_ref[...].astype(EIGHT)

    def scores(vectors, vectors_low):
        terms = lax.dot_general(vectors[...], parts_ref[...], NT, preferred_element_type=jnp.float32)
        rest = lax.dot_general(vectors_low[...], eighth_ref[...], NT, preferred_element_type=jnp.float32)
        return terms[:, :TILE] + (terms[:, TILE:] + rest * (1 / SCALE))

    best = [jnp.full((1, TILE), LOWEST, jnp.float32) for _ in range(1 + places_ref.shape[0])]
    for side in range(2):
        centers_ref, centers_low_ref, counts_ref, vectors_ref, vectors_low_ref = halves[5 * side : 5 * side + 5]
        lists, length = vectors_ref.shape[:2]
        place = lax.broadcasted_iota(jnp.int32, (length, TILE), 0)
        best[0] = jnp.maximum(best[0], jnp.max(scores(centers_ref, centers_low_ref), axis=0, keepdims=True))
        for slot in range(lists):
            usable = jnp.where(place < counts_ref[pl.ds(slot, 1), :], scores(vectors_ref.at[slot], vectors_low_ref.at[slot]), LOWEST)
            found = jnp.max(usable, axis=0, keepdims=True)
            for step in range(places_ref.shape[0]):
                chosen = jnp.where(places_ref[pl.ds(step, 1), :] == slot, found, LOWEST)
                best[1 + step] = jnp.maximum(best[1 + step], chosen)
    best = [pltpu.roll(row, kind * rows_dev, 1) if kind else row for kind, row in enumerate(best)]
    lane_chip = lax.broadcasted_iota(jnp.int32, (1, TILE), 1) // rows_dev
    nothing = jnp.full((1, TILE), LOWEST, jnp.float32)
    for chip in range(chunks):
        row = best[0]
        for kind in range(1, len(best)):
            row = jnp.where(lane_chip == (chip + kind) % chunks, best[kind], row)
        straight = crossed((pl.program_id(0) * chunks + chip) ^ origin) == (here() & 1)
        out_ref[2 * chip] = jnp.where(straight, row, nothing)
        out_ref[2 * chip + 1] = jnp.where(straight, nothing, row)


def score(rows_dev, blocks, places, *halves):
    half, depth = blocks.shape
    kinds = 1 + places.shape[0]
    rows = 2 * (halves[0].shape[0] + halves[3].shape[0] * halves[3].shape[1])
    devices = 2 * TILE // rows_dev
    return pl.pallas_call(
        functools.partial(score_kernel, rows_dev=rows_dev),
        out_shape=jax.ShapeDtypeStruct((half // TILE * devices, 1, TILE), jnp.float32),
        grid=(half // TILE,),
        in_specs=[WHOLE, pl.BlockSpec((kinds - 1, TILE), lambda i: (0, i)), *[WHOLE] * len(halves)],
        out_specs=pl.BlockSpec((devices, 1, TILE), lambda i: (i, 0, 0)),
        scratch_shapes=[
            pltpu.VMEM((TILE, depth), jnp.float32),
            pltpu.VMEM((2 * TILE, depth), jnp.bfloat16),
            pltpu.VMEM((TILE, depth), EIGHT),
        ],
        compiler_params=pltpu.CompilerParams(vmem_limit_bytes=LARGE),
        cost_estimate=pl.CostEstimate(flops=8 * rows * half * depth, bytes_accessed=4 * rows * depth, transcendentals=0),
        name="score",
    )(blocks, places, *halves)


def finish_kernel(arrived_ref, coarse_ref, fine_ref, *, rows_dev):
    best = jnp.max(arrived_ref[...], axis=0)
    lane = ((here() >> 1) * rows_dev) % TILE
    best = pltpu.roll(best, (TILE - lane) % TILE, 1)
    coarse_ref[...] = best[0, :rows_dev]
    for step in range(fine_ref.shape[0]):
        fine_ref[pl.ds(step, 1), :] = best[:, (1 + step) * rows_dev : (2 + step) * rows_dev]


def finish(rows_dev, steps, arrived):
    return pl.pallas_call(
        functools.partial(finish_kernel, rows_dev=rows_dev),
        out_shape=(
            jax.ShapeDtypeStruct((rows_dev,), jnp.float32),
            jax.ShapeDtypeStruct((steps, rows_dev), jnp.float32),
        ),
        in_specs=[WHOLE],
        out_specs=(WHOLE, WHOLE),
        compiler_params=pltpu.CompilerParams(vmem_limit_bytes=SMALL),
        name="finish",
    )(arrived)


def gathered(blocks, stage):
    return [exchanged(blocks, mask) for mask in stage]


def in_hbm(*arrays):
    return [pltpu.with_memory_space_constraint(array, pltpu.HBM) for array in arrays]


def local(queries, centroids, stored, vector_ids, list_home, probes):
    devices = lax.axis_size("group") * lax.axis_size("member")
    rows_dev, lists = queries.shape[0], stored.shape[0]
    first, *rest = stages()
    arrived = gathered(queries, first)
    mine = (centroids, vector_ids, stored)
    theirs = [exchanged(array, 1) for array in mine]
    places, copied = lookup(devices // 2 * rows_dev, lists, *in_hbm(list_home, probes.transpose(1, 0, 2), queries))
    blocks = jnp.concatenate([copied, *arrived], axis=0)
    for number, stage in enumerate(rest):
        if number == len(rest) - 1:
            blocks, places, *mine = lax.optimization_barrier((blocks, places, *mine))
        arrived = gathered(blocks, stage)
        if number == len(rest) - 1:
            ready = prepare(*in_hbm(*mine), True), prepare(*theirs, False)
            arrived, ready = lax.optimization_barrier((arrived, ready))
        blocks = jnp.concatenate([blocks, *arrived], axis=0)
    parts = score(rows_dev, blocks, places, *ready[0], *ready[1])
    return finish(rows_dev, probes.shape[1], lax.all_to_all(parts, BOTH, 0, 0, tiled=True))


def solution(mesh):
    placed = (
        P(BOTH, None),
        P(BOTH, None),
        P("group", "member", None),
        P("group", "member"),
        P(),
        P(),
    )
    return jax.shard_map(
        local,
        mesh=mesh,
        in_specs=placed,
        out_specs=(P(BOTH), P(None, BOTH)),
        check_vma=False,
    )
```

```python
import functools

import jax
import jax.numpy as jnp
from jax import lax
from jax.experimental import pallas as pl
from jax.experimental.pallas import tpu as pltpu
from jax.sharding import PartitionSpec as P

LOWEST = -1e30
TILE = 128
EIGHT = jnp.float8_e4m3fn
SCALE = 2.0**16
BOTH = ("group", "member")
NT = (((1,), (1,)), ((), ()))
LARGE = 20 * 2**20
SMALL = 10 * 2**20
WHOLE = pl.BlockSpec(memory_space=pltpu.VMEM)
ANYWHERE = pl.BlockSpec(memory_space=pl.ANY)


def parity(index):
    return bin(index).count("1") % 2


def stages():
    members, groups = lax.axis_size("member"), lax.axis_size("group")
    inner = [1 << k for k in range(1, members.bit_length() - 1)]
    outer = [members << k for k in range(groups.bit_length() - 1)]
    pairs = [bits[at : at + 2] for bits in (inner, outer) for at in range(0, len(bits), 2)]
    mirrored = pairs[::-1] if [len(p) for p in pairs] == [len(p) for p in pairs[::-1]] else pairs

    def masks(pair, last):
        order = (2, 1, 3) if pair[0] < members else (1, 3, 2) if last else (3, 1, 2)
        chosen = [pair[0] * value for value in order] if len(pair) == 2 else pair
        return [mask | parity(mask) for mask in chosen]

    count = len(pairs)
    return [list(zip(masks(pairs[k], k == count - 1), masks(mirrored[k], k == count - 1))) for k in range(count)]


def exchanged(value, masks):
    devices = lax.axis_size("group") * lax.axis_size("member")
    return lax.ppermute(value, BOTH, [(d, d ^ masks[parity(d)]) for d in range(devices)])


def position(chip, odd):
    offsets = [0]
    for stage in stages():
        offsets = [offset ^ (mask >> 1) for mask in [0, *[masks[odd] for masks in stage]] for offset in offsets]
    place = 0
    for k in range(len(offsets).bit_length() - 1):
        place = place ^ (((chip >> k) & 1) * offsets.index(1 << k))
    return place


def here():
    return lax.axis_index("group") * lax.axis_size("member") + lax.axis_index("member")


def parity_of(index, count):
    found = 0
    for k in range(count.bit_length() - 1):
        found = found ^ ((index >> k) & 1)
    return found


def split(value):
    high = value.astype(jnp.bfloat16)
    return high, value - high.astype(jnp.float32)


def copy_all(pairs, sems):
    copies = [pltpu.make_async_copy(source, target, sems.at[k]) for k, (source, target) in enumerate(pairs)]
    for copy in copies:
        copy.start()
    return copies


def lookup_kernel(home_hbm, probes_hbm, queries_hbm, places_ref, queries_ref, home_ref, probes_ref, sems, *, lists, lanes):
    copies = copy_all([(home_hbm, home_ref), (probes_hbm, probes_ref), (queries_hbm, queries_ref)], sems)
    copies[0].wait()
    copies[1].wait()
    group = lax.axis_index("group")
    steps, blocks, probed = probes_ref.shape
    lane_block = lax.broadcasted_iota(jnp.int32, (1, places_ref.shape[1]), 1) // lanes
    for step in range(steps):

        def of_block(b, row, step=step):
            place = jnp.int32(-1)
            for j in range(probed):
                slot = home_ref[probes_ref[step, b, j]]
                place = jnp.where(slot // lists == group, slot % lists, place)
            return jnp.where(lane_block == b, place, row)

        row = jnp.full(lane_block.shape, -1, jnp.int32)
        places_ref[pl.ds(step, 1), :] = lax.fori_loop(0, blocks, of_block, row)
    copies[2].wait()


def lookup(half, lists, list_home, probes, queries):
    steps, blocks, _ = probes.shape
    return pl.pallas_call(
        functools.partial(lookup_kernel, lists=lists, lanes=half // blocks),
        out_shape=(
            jax.ShapeDtypeStruct((steps, half), jnp.int32),
            jax.ShapeDtypeStruct(queries.shape, queries.dtype),
        ),
        in_specs=[ANYWHERE] * 3,
        out_specs=(WHOLE, WHOLE),
        scratch_shapes=[
            pltpu.SMEM(list_home.shape, jnp.int32),
            pltpu.SMEM(probes.shape, jnp.int32),
            pltpu.SemaphoreType.DMA((3,)),
        ],
        compiler_params=pltpu.CompilerParams(vmem_limit_bytes=SMALL),
        cost_estimate=pl.CostEstimate(flops=10000, bytes_accessed=100000, transcendentals=0),
        name="lookup",
    )(list_home, probes, queries)


def split_vectors(value):
    high, low = split(value)
    return high, (low * SCALE).astype(EIGHT)


def split_lists(centroids_ref, ids_ref, stored_ref, *refs, arrived=lambda k: None):
    centers_ref, centers_low_ref, counts_ref, vectors_ref, vectors_low_ref = refs
    arrived(0)
    arrived(1)
    centers_ref[...], centers_low_ref[...] = split_vectors(centroids_ref[...])
    valid = jnp.sum((ids_ref[...] >= 0).astype(jnp.float32), axis=1, keepdims=True)
    counts_ref[...] = jnp.broadcast_to(valid, counts_ref.shape).astype(jnp.int32)
    for k in range(stored_ref.shape[0]):
        arrived(2 + k)
        vectors_ref[k], vectors_low_ref[k] = split_vectors(stored_ref[k])


def copied_kernel(centroids_hbm, ids_hbm, stored_hbm, *refs):
    *outs, centroids_ref, ids_ref, stored_ref, sems = refs
    lists = stored_ref.shape[0]
    pairs = [(centroids_hbm, centroids_ref), (ids_hbm, ids_ref), *[(stored_hbm.at[k], stored_ref.at[k]) for k in range(lists)]]
    copies = copy_all(pairs, sems)
    split_lists(centroids_ref, ids_ref, stored_ref, *outs, arrived=lambda k: copies[k].wait())


def prepare(centroids, ids, stored, copied):
    lists, length, depth = stored.shape
    rows = lists * length + centroids.shape[0]
    scratch = [pltpu.VMEM(array.shape, array.dtype) for array in (centroids, ids, stored)]
    return pl.pallas_call(
        copied_kernel if copied else split_lists,
        out_shape=(
            jax.ShapeDtypeStruct(centroids.shape, jnp.bfloat16),
            jax.ShapeDtypeStruct(centroids.shape, EIGHT),
            jax.ShapeDtypeStruct((lists, TILE), jnp.int32),
            jax.ShapeDtypeStruct(stored.shape, jnp.bfloat16),
            jax.ShapeDtypeStruct(stored.shape, EIGHT),
        ),
        in_specs=[ANYWHERE if copied else WHOLE] * 3,
        out_specs=(WHOLE,) * 5,
        scratch_shapes=[*scratch, pltpu.SemaphoreType.DMA((2 + lists,))] if copied else [],
        compiler_params=pltpu.CompilerParams(vmem_limit_bytes=SMALL),
        cost_estimate=pl.CostEstimate(flops=6 * rows * depth, bytes_accessed=8 * rows * depth, transcendentals=0),
        name="prepare",
    )(centroids, ids, stored)


def score_kernel(blocks_ref, places_ref, *refs, rows_dev):
    *halves, out_ref, queries_ref, parts_ref, eighth_ref = refs
    devices = lax.axis_size("group") * lax.axis_size("member")
    odd = parity_of(here(), devices)
    chunks = TILE // rows_dev

    def place_of(chip):
        return jnp.where(odd == 1, position(chip, 1), position(chip, 0))

    first = place_of(here() >> 1)
    for chunk in range(chunks):
        offset = place_of(chunk if blocks_ref.shape[0] == TILE else pl.program_id(0) * chunks + chunk)
        source = pl.multiple_of((first ^ offset) * rows_dev, rows_dev)
        queries_ref[pl.ds(chunk * rows_dev, rows_dev), :] = blocks_ref[pl.ds(source, rows_dev), :]
    high, low = split(queries_ref[...])
    parts_ref[:TILE], parts_ref[TILE:] = high, low.astype(jnp.bfloat16)
    eighth_ref[...] = queries_ref[...].astype(EIGHT)

    def scores(vectors, vectors_low):
        terms = lax.dot_general(vectors[...], parts_ref[...], NT, preferred_element_type=jnp.float32)
        rest = lax.dot_general(vectors_low[...], eighth_ref[...], NT, preferred_element_type=jnp.float32)
        return terms[:, :TILE] + (terms[:, TILE:] + rest * (1 / SCALE))

    best = [jnp.full((1, TILE), LOWEST, jnp.float32) for _ in range(1 + places_ref.shape[0])]
    for side in range(2):
        centers_ref, centers_low_ref, counts_ref, vectors_ref, vectors_low_ref = halves[5 * side : 5 * side + 5]
        lists, length = vectors_ref.shape[:2]
        place = lax.broadcasted_iota(jnp.int32, (length, TILE), 0)
        best[0] = jnp.maximum(best[0], jnp.max(scores(centers_ref, centers_low_ref), axis=0, keepdims=True))
        for slot in range(lists):
            usable = jnp.where(place < counts_ref[pl.ds(slot, 1), :], scores(vectors_ref.at[slot], vectors_low_ref.at[slot]), LOWEST)
            found = jnp.max(usable, axis=0, keepdims=True)
            for step in range(places_ref.shape[0]):
                chosen = jnp.where(places_ref[pl.ds(step, 1), :] == slot, found, LOWEST)
                best[1 + step] = jnp.maximum(best[1 + step], chosen)
    best = [pltpu.roll(row, kind * rows_dev, 1) if kind else row for kind, row in enumerate(best)]
    lane_chip = lax.broadcasted_iota(jnp.int32, (1, TILE), 1) // rows_dev
    nothing = jnp.full((1, TILE), LOWEST, jnp.float32)
    for chip in range(chunks):
        row = best[0]
        for kind in range(1, len(best)):
            row = jnp.where(lane_chip == (chip + kind) % chunks, best[kind], row)
        straight = odd == parity_of(pl.program_id(0), devices) ^ parity(chip)
        out_ref[2 * chip] = jnp.where(straight, row, nothing)
        out_ref[2 * chip + 1] = jnp.where(straight, nothing, row)


def score(rows_dev, blocks, places, *halves):
    half, depth = blocks.shape
    kinds = 1 + places.shape[0]
    rows = 2 * (halves[0].shape[0] + halves[3].shape[0] * halves[3].shape[1])
    devices = 2 * TILE // rows_dev
    return pl.pallas_call(
        functools.partial(score_kernel, rows_dev=rows_dev),
        out_shape=jax.ShapeDtypeStruct((half // TILE * devices, 1, TILE), jnp.float32),
        grid=(half // TILE,),
        in_specs=[WHOLE, pl.BlockSpec((kinds - 1, TILE), lambda i: (0, i)), *[WHOLE] * len(halves)],
        out_specs=pl.BlockSpec((devices, 1, TILE), lambda i: (i, 0, 0)),
        scratch_shapes=[
            pltpu.VMEM((TILE, depth), jnp.float32),
            pltpu.VMEM((2 * TILE, depth), jnp.bfloat16),
            pltpu.VMEM((TILE, depth), EIGHT),
        ],
        compiler_params=pltpu.CompilerParams(vmem_limit_bytes=LARGE),
        cost_estimate=pl.CostEstimate(flops=8 * rows * half * depth, bytes_accessed=4 * rows * depth, transcendentals=0),
        name="score",
    )(blocks, places, *halves)


def finish_kernel(arrived_ref, coarse_ref, fine_ref, *, rows_dev):
    best = jnp.max(arrived_ref[...], axis=0)
    lane = ((here() >> 1) * rows_dev) % TILE
    best = pltpu.roll(best, (TILE - lane) % TILE, 1)
    coarse_ref[...] = best[0, :rows_dev]
    for step in range(fine_ref.shape[0]):
        fine_ref[pl.ds(step, 1), :] = best[:, (1 + step) * rows_dev : (2 + step) * rows_dev]


def finish(rows_dev, steps, arrived):
    return pl.pallas_call(
        functools.partial(finish_kernel, rows_dev=rows_dev),
        out_shape=(
            jax.ShapeDtypeStruct((rows_dev,), jnp.float32),
            jax.ShapeDtypeStruct((steps, rows_dev), jnp.float32),
        ),
        in_specs=[WHOLE],
        out_specs=(WHOLE, WHOLE),
        compiler_params=pltpu.CompilerParams(vmem_limit_bytes=SMALL),
        name="finish",
    )(arrived)


def gathered(blocks, stage):
    return [exchanged(blocks, masks) for masks in stage]


def in_hbm(*arrays):
    return [pltpu.with_memory_space_constraint(array, pltpu.HBM) for array in arrays]


def local(queries, centroids, stored, vector_ids, list_home, probes):
    devices = lax.axis_size("group") * lax.axis_size("member")
    rows_dev, lists = queries.shape[0], stored.shape[0]
    first, *rest = stages()
    arrived = gathered(queries, first)
    mine = (centroids, vector_ids, stored)
    theirs = [exchanged(array, (1, 1)) for array in mine]
    places, copied = lookup(devices // 2 * rows_dev, lists, *in_hbm(list_home, probes.transpose(1, 0, 2), queries))
    blocks = jnp.concatenate([copied, *arrived], axis=0)
    for number, stage in enumerate(rest):
        if number == len(rest) - 1:
            blocks, places, *mine = lax.optimization_barrier((blocks, places, *mine))
        arrived = gathered(blocks, stage)
        if number == len(rest) - 1:
            ready = prepare(*in_hbm(*mine), True), prepare(*theirs, False)
            arrived, ready = lax.optimization_barrier((arrived, ready))
        blocks = jnp.concatenate([blocks, *arrived], axis=0)
    parts = score(rows_dev, blocks, places, *ready[0], *ready[1])
    return finish(rows_dev, probes.shape[1], lax.all_to_all(parts, BOTH, 0, 0, tiled=True))


def solution(mesh):
    placed = (
        P(BOTH, None),
        P(BOTH, None),
        P("group", "member", None),
        P("group", "member"),
        P(),
        P(),
    )
    return jax.shard_map(
        local,
        mesh=mesh,
        in_specs=placed,
        out_specs=(P(BOTH), P(None, BOTH)),
        check_vma=False,
    )
```

```python
import functools

import jax
import jax.numpy as jnp
from jax import lax
from jax.experimental import pallas as pl
from jax.experimental.pallas import tpu as pltpu
from jax.sharding import PartitionSpec as P

LOWEST = -1e30
TILE = 128
EIGHT = jnp.float8_e4m3fn
SCALE = 2.0**16
BOTH = ("group", "member")
NT = (((1,), (1,)), ((), ()))
LARGE = 20 * 2**20
SMALL = 10 * 2**20
WHOLE = pl.BlockSpec(memory_space=pltpu.VMEM)
ANYWHERE = pl.BlockSpec(memory_space=pl.ANY)


def parity(index):
    return bin(index).count("1") % 2


def stages():
    members, groups = lax.axis_size("member"), lax.axis_size("group")
    inner = [1 << k for k in range(1, members.bit_length() - 1)]
    outer = [members << k for k in range(groups.bit_length() - 1)]
    pairs = [bits[at : at + 2] for bits in (inner, outer) for at in range(0, len(bits), 2)]
    mirrored = pairs[::-1] if [len(p) for p in pairs] == [len(p) for p in pairs[::-1]] else pairs

    def masks(pair, last):
        order = (2, 1, 3) if pair[0] < members else (1, 3, 2) if last else (3, 1, 2)
        chosen = [pair[0] * value for value in order] if len(pair) == 2 else pair
        return [mask | parity(mask) for mask in chosen]

    count = len(pairs)
    return [list(zip(masks(pairs[k], k == count - 1), masks(mirrored[k], k == count - 1))) for k in range(count)]


def exchanged(value, masks):
    devices = lax.axis_size("group") * lax.axis_size("member")
    return lax.ppermute(value, BOTH, [(d, d ^ masks[parity(d)]) for d in range(devices)])


def position(chip, odd):
    offsets = [0]
    for stage in stages():
        offsets = [offset ^ (mask >> 1) for mask in [0, *[masks[odd] for masks in stage]] for offset in offsets]
    place = 0
    for k in range(len(offsets).bit_length() - 1):
        place = place ^ (((chip >> k) & 1) * offsets.index(1 << k))
    return place


def here():
    return lax.axis_index("group") * lax.axis_size("member") + lax.axis_index("member")


def parity_of(index, count):
    found = 0
    for k in range(count.bit_length() - 1):
        found = found ^ ((index >> k) & 1)
    return found


def split(value):
    high = value.astype(jnp.bfloat16)
    return high, value - high.astype(jnp.float32)


def copy_all(pairs, sems):
    copies = [pltpu.make_async_copy(source, target, sems.at[k]) for k, (source, target) in enumerate(pairs)]
    for copy in copies:
        copy.start()
    return copies


def lookup_kernel(home_hbm, probes_hbm, queries_hbm, places_ref, queries_ref, home_ref, probes_ref, sems, *, lists, lanes):
    copies = copy_all([(home_hbm, home_ref), (probes_hbm, probes_ref), (queries_hbm, queries_ref)], sems)
    copies[0].wait()
    copies[1].wait()
    group = lax.axis_index("group")
    steps, blocks, probed = probes_ref.shape
    lane_block = lax.broadcasted_iota(jnp.int32, (1, places_ref.shape[1]), 1) // lanes
    for step in range(steps):

        def of_block(b, row, step=step):
            place = jnp.int32(-1)
            for j in range(probed):
                slot = home_ref[probes_ref[step, b, j]]
                place = jnp.where(slot // lists == group, slot % lists, place)
            return jnp.where(lane_block == b, place, row)

        row = jnp.full(lane_block.shape, -1, jnp.int32)
        places_ref[pl.ds(step, 1), :] = lax.fori_loop(0, blocks, of_block, row)
    copies[2].wait()


def lookup(half, lists, list_home, probes, queries):
    steps, blocks, _ = probes.shape
    return pl.pallas_call(
        functools.partial(lookup_kernel, lists=lists, lanes=half // blocks),
        out_shape=(
            jax.ShapeDtypeStruct((steps, half), jnp.int32),
            jax.ShapeDtypeStruct(queries.shape, queries.dtype),
        ),
        in_specs=[ANYWHERE] * 3,
        out_specs=(WHOLE, WHOLE),
        scratch_shapes=[
            pltpu.SMEM(list_home.shape, jnp.int32),
            pltpu.SMEM(probes.shape, jnp.int32),
            pltpu.SemaphoreType.DMA((3,)),
        ],
        compiler_params=pltpu.CompilerParams(vmem_limit_bytes=SMALL),
        cost_estimate=pl.CostEstimate(flops=10000, bytes_accessed=100000, transcendentals=0),
        name="lookup",
    )(list_home, probes, queries)


def split_vectors(value):
    high, low = split(value)
    return high, (low * SCALE).astype(EIGHT)


def split_lists(centroids_ref, ids_ref, stored_ref, *refs, arrived=lambda k: None):
    centers_ref, centers_low_ref, counts_ref, vectors_ref, vectors_low_ref = refs
    arrived(0)
    arrived(1)
    centers_ref[...], centers_low_ref[...] = split_vectors(centroids_ref[...])
    valid = jnp.sum((ids_ref[...] >= 0).astype(jnp.float32), axis=1, keepdims=True)
    counts_ref[...] = jnp.broadcast_to(valid, counts_ref.shape).astype(jnp.int32)
    for k in range(stored_ref.shape[0]):
        arrived(2 + k)
        vectors_ref[k], vectors_low_ref[k] = split_vectors(stored_ref[k])


def copied_kernel(centroids_hbm, ids_hbm, stored_hbm, *refs):
    *outs, centroids_ref, ids_ref, stored_ref, sems = refs
    lists = stored_ref.shape[0]
    pairs = [(centroids_hbm, centroids_ref), (ids_hbm, ids_ref), *[(stored_hbm.at[k], stored_ref.at[k]) for k in range(lists)]]
    copies = copy_all(pairs, sems)
    split_lists(centroids_ref, ids_ref, stored_ref, *outs, arrived=lambda k: copies[k].wait())


def prepare(centroids, ids, stored, copied):
    lists, length, depth = stored.shape
    rows = lists * length + centroids.shape[0]
    scratch = [pltpu.VMEM(array.shape, array.dtype) for array in (centroids, ids, stored)]
    return pl.pallas_call(
        copied_kernel if copied else split_lists,
        out_shape=(
            jax.ShapeDtypeStruct(centroids.shape, jnp.bfloat16),
            jax.ShapeDtypeStruct(centroids.shape, EIGHT),
            jax.ShapeDtypeStruct((lists, TILE), jnp.int32),
            jax.ShapeDtypeStruct(stored.shape, jnp.bfloat16),
            jax.ShapeDtypeStruct(stored.shape, EIGHT),
        ),
        in_specs=[ANYWHERE if copied else WHOLE] * 3,
        out_specs=(WHOLE,) * 5,
        scratch_shapes=[*scratch, pltpu.SemaphoreType.DMA((2 + lists,))] if copied else [],
        compiler_params=pltpu.CompilerParams(vmem_limit_bytes=SMALL),
        cost_estimate=pl.CostEstimate(flops=6 * rows * depth, bytes_accessed=8 * rows * depth, transcendentals=0),
        name="prepare",
    )(centroids, ids, stored)


def score_kernel(blocks_ref, places_ref, *refs, rows_dev):
    *halves, out_ref, queries_ref, parts_ref, eighth_ref = refs
    devices = lax.axis_size("group") * lax.axis_size("member")
    odd = parity_of(here(), devices)
    chunks = TILE // rows_dev

    def place_of(chip):
        return jnp.where(odd == 1, position(chip, 1), position(chip, 0))

    first = place_of(here() >> 1)
    for chunk in range(chunks):
        offset = place_of(chunk if blocks_ref.shape[0] == TILE else pl.program_id(0) * chunks + chunk)
        source = pl.multiple_of((first ^ offset) * rows_dev, rows_dev)
        queries_ref[pl.ds(chunk * rows_dev, rows_dev), :] = blocks_ref[pl.ds(source, rows_dev), :]
    high, low = split(queries_ref[...])
    parts_ref[:TILE], parts_ref[TILE:] = high, low.astype(jnp.bfloat16)
    eighth_ref[...] = queries_ref[...].astype(EIGHT)

    def scores(vectors, vectors_low):
        terms = lax.dot_general(vectors[...], parts_ref[...], NT, preferred_element_type=jnp.float32)
        rest = lax.dot_general(vectors_low[...], eighth_ref[...], NT, preferred_element_type=jnp.float32)
        return terms[:, :TILE] + (terms[:, TILE:] + rest * (1 / SCALE))

    best = [jnp.full((1, TILE), LOWEST, jnp.float32) for _ in range(1 + places_ref.shape[0])]
    for side in range(2):
        centers_ref, centers_low_ref, counts_ref, vectors_ref, vectors_low_ref = halves[5 * side : 5 * side + 5]
        lists, length = vectors_ref.shape[:2]
        place = lax.broadcasted_iota(jnp.int32, (length, TILE), 0)
        for slot in range(lists):
            high, low = vectors_ref[slot], vectors_low_ref[slot]
            if side == 1 and slot == lists - 1:
                high = jnp.concatenate([high, halves[0][...], centers_ref[...]], axis=0)
                low = jnp.concatenate([low, halves[1][...], centers_low_ref[...]], axis=0)
            found = scores(high, low)
            if side == 1 and slot == lists - 1:
                best[0] = jnp.max(found[length:], axis=0, keepdims=True)
            usable = jnp.where(place < counts_ref[pl.ds(slot, 1), :], found[:length], LOWEST)
            found = jnp.max(usable, axis=0, keepdims=True)
            for step in range(places_ref.shape[0]):
                chosen = jnp.where(places_ref[pl.ds(step, 1), :] == slot, found, LOWEST)
                best[1 + step] = jnp.maximum(best[1 + step], chosen)
    best = [pltpu.roll(row, kind * rows_dev, 1) if kind else row for kind, row in enumerate(best)]
    lane_chip = lax.broadcasted_iota(jnp.int32, (1, TILE), 1) // rows_dev
    nothing = jnp.full((1, TILE), LOWEST, jnp.float32)
    for chip in range(chunks):
        row = best[0]
        for kind in range(1, len(best)):
            row = jnp.where(lane_chip == (chip + kind) % chunks, best[kind], row)
        straight = odd == parity_of(pl.program_id(0), devices) ^ parity(chip)
        out_ref[2 * chip] = jnp.where(straight, row, nothing)
        out_ref[2 * chip + 1] = jnp.where(straight, nothing, row)


def score(rows_dev, blocks, places, *halves):
    half, depth = blocks.shape
    kinds = 1 + places.shape[0]
    rows = 2 * (halves[0].shape[0] + halves[3].shape[0] * halves[3].shape[1])
    devices = 2 * TILE // rows_dev
    return pl.pallas_call(
        functools.partial(score_kernel, rows_dev=rows_dev),
        out_shape=jax.ShapeDtypeStruct((half // TILE * devices, 1, TILE), jnp.float32),
        grid=(half // TILE,),
        in_specs=[WHOLE, pl.BlockSpec((kinds - 1, TILE), lambda i: (0, i)), *[WHOLE] * len(halves)],
        out_specs=pl.BlockSpec((devices, 1, TILE), lambda i: (i, 0, 0)),
        scratch_shapes=[
            pltpu.VMEM((TILE, depth), jnp.float32),
            pltpu.VMEM((2 * TILE, depth), jnp.bfloat16),
            pltpu.VMEM((TILE, depth), EIGHT),
        ],
        compiler_params=pltpu.CompilerParams(vmem_limit_bytes=LARGE),
        cost_estimate=pl.CostEstimate(flops=8 * rows * half * depth, bytes_accessed=4 * rows * depth, transcendentals=0),
        name="score",
    )(blocks, places, *halves)


def finish_kernel(arrived_ref, coarse_ref, fine_ref, *, rows_dev):
    best = jnp.max(arrived_ref[...], axis=0)
    lane = ((here() >> 1) * rows_dev) % TILE
    best = pltpu.roll(best, (TILE - lane) % TILE, 1)
    coarse_ref[...] = best[0, :rows_dev]
    for step in range(fine_ref.shape[0]):
        fine_ref[pl.ds(step, 1), :] = best[:, (1 + step) * rows_dev : (2 + step) * rows_dev]


def finish(rows_dev, steps, arrived):
    return pl.pallas_call(
        functools.partial(finish_kernel, rows_dev=rows_dev),
        out_shape=(
            jax.ShapeDtypeStruct((rows_dev,), jnp.float32),
            jax.ShapeDtypeStruct((steps, rows_dev), jnp.float32),
        ),
        in_specs=[WHOLE],
        out_specs=(WHOLE, WHOLE),
        compiler_params=pltpu.CompilerParams(vmem_limit_bytes=SMALL),
        name="finish",
    )(arrived)


def gathered(blocks, stage):
    return [exchanged(blocks, masks) for masks in stage]


def in_hbm(*arrays):
    return [pltpu.with_memory_space_constraint(array, pltpu.HBM) for array in arrays]


def local(queries, centroids, stored, vector_ids, list_home, probes):
    devices = lax.axis_size("group") * lax.axis_size("member")
    rows_dev, lists = queries.shape[0], stored.shape[0]
    first, *rest = stages()
    arrived = gathered(queries, first)
    mine = (centroids, vector_ids, stored)
    theirs = [exchanged(array, (1, 1)) for array in mine]
    places, copied = lookup(devices // 2 * rows_dev, lists, *in_hbm(list_home, probes.transpose(1, 0, 2), queries))
    blocks = jnp.concatenate([copied, *arrived], axis=0)
    for number, stage in enumerate(rest):
        if number == len(rest) - 1:
            blocks, places, *mine = lax.optimization_barrier((blocks, places, *mine))
        arrived = gathered(blocks, stage)
        if number == len(rest) - 1:
            ready = prepare(*in_hbm(*mine), True), prepare(*theirs, False)
            arrived, ready = lax.optimization_barrier((arrived, ready))
        blocks = jnp.concatenate([blocks, *arrived], axis=0)
    parts = score(rows_dev, blocks, places, *ready[0], *ready[1])
    return finish(rows_dev, probes.shape[1], lax.all_to_all(parts, BOTH, 0, 0, tiled=True))


def solution(mesh):
    placed = (
        P(BOTH, None),
        P(BOTH, None),
        P("group", "member", None),
        P("group", "member"),
        P(),
        P(),
    )
    return jax.shard_map(
        local,
        mesh=mesh,
        in_specs=placed,
        out_specs=(P(BOTH), P(None, BOTH)),
        check_vma=False,
    )
```

```python
import functools

import jax
import jax.numpy as jnp
from jax import lax
from jax.experimental import pallas as pl
from jax.experimental.pallas import tpu as pltpu
from jax.sharding import PartitionSpec as P

LOWEST = -1e30
TILE = 128
EIGHT = jnp.float8_e4m3fn
SCALE = 2.0**16
BOTH = ("group", "member")
NT = (((1,), (1,)), ((), ()))
LARGE = 20 * 2**20
SMALL = 10 * 2**20
WHOLE = pl.BlockSpec(memory_space=pltpu.VMEM)
ANYWHERE = pl.BlockSpec(memory_space=pl.ANY)


def parity(index):
    return bin(index).count("1") % 2


def stages():
    members, groups = lax.axis_size("member"), lax.axis_size("group")
    inner = [1 << k for k in range(1, members.bit_length() - 1)]
    outer = [members << k for k in range(groups.bit_length() - 1)]
    pairs = [bits[at : at + 2] for bits in (inner, outer) for at in range(0, len(bits), 2)]
    mirrored = pairs[::-1] if [len(p) for p in pairs] == [len(p) for p in pairs[::-1]] else pairs

    def masks(pair, last):
        order = (2, 1, 3) if pair[0] < members else (1, 3, 2) if last else (3, 1, 2)
        chosen = [pair[0] * value for value in order] if len(pair) == 2 else pair
        return [mask | parity(mask) for mask in chosen]

    count = len(pairs)
    return [list(zip(masks(pairs[k], k == count - 1), masks(mirrored[k], k == count - 1))) for k in range(count)]


def exchanged(value, masks):
    devices = lax.axis_size("group") * lax.axis_size("member")
    return lax.ppermute(value, BOTH, [(d, d ^ masks[parity(d)]) for d in range(devices)])


def position(chip, odd):
    offsets = [0]
    for stage in stages():
        offsets = [offset ^ (mask >> 1) for mask in [0, *[masks[odd] for masks in stage]] for offset in offsets]
    place = 0
    for k in range(len(offsets).bit_length() - 1):
        place = place ^ (((chip >> k) & 1) * offsets.index(1 << k))
    return place


def here():
    return lax.axis_index("group") * lax.axis_size("member") + lax.axis_index("member")


def parity_of(index, count):
    found = 0
    for k in range(count.bit_length() - 1):
        found = found ^ ((index >> k) & 1)
    return found


def split(value):
    high = value.astype(jnp.bfloat16)
    return high, value - high.astype(jnp.float32)


def copy_all(pairs, sems):
    copies = [pltpu.make_async_copy(source, target, sems.at[k]) for k, (source, target) in enumerate(pairs)]
    for copy in copies:
        copy.start()
    return copies


def lookup_kernel(home_hbm, probes_hbm, queries_hbm, places_ref, queries_ref, home_ref, probes_ref, sems, *, lists, lanes):
    copies = copy_all([(home_hbm, home_ref), (probes_hbm, probes_ref), (queries_hbm, queries_ref)], sems)
    copies[0].wait()
    copies[1].wait()
    group = lax.axis_index("group")
    steps, blocks, probed = probes_ref.shape
    lane_block = lax.broadcasted_iota(jnp.int32, (1, places_ref.shape[1]), 1) // lanes
    for step in range(steps):

        def of_block(b, row, step=step):
            place = jnp.int32(-1)
            for j in range(probed):
                slot = home_ref[probes_ref[step, b, j]]
                place = jnp.where(slot // lists == group, slot % lists, place)
            return jnp.where(lane_block == b, place, row)

        row = jnp.full(lane_block.shape, -1, jnp.int32)
        places_ref[pl.ds(step, 1), :] = lax.fori_loop(0, blocks, of_block, row)
    copies[2].wait()


def lookup(half, lists, list_home, probes, queries):
    steps, blocks, _ = probes.shape
    return pl.pallas_call(
        functools.partial(lookup_kernel, lists=lists, lanes=half // blocks),
        out_shape=(
            jax.ShapeDtypeStruct((steps, half), jnp.int32),
            jax.ShapeDtypeStruct(queries.shape, queries.dtype),
        ),
        in_specs=[ANYWHERE] * 3,
        out_specs=(WHOLE, WHOLE),
        scratch_shapes=[
            pltpu.SMEM(list_home.shape, jnp.int32),
            pltpu.SMEM(probes.shape, jnp.int32),
            pltpu.SemaphoreType.DMA((3,)),
        ],
        compiler_params=pltpu.CompilerParams(vmem_limit_bytes=SMALL),
        cost_estimate=pl.CostEstimate(flops=10000, bytes_accessed=100000, transcendentals=0),
        name="lookup",
    )(list_home, probes, queries)


def split_vectors(value):
    high, low = split(value)
    return high, (low * SCALE).astype(EIGHT)


def split_lists(centroids_ref, ids_ref, stored_ref, *refs, arrived=lambda k: None):
    centers_ref, centers_low_ref, counts_ref, vectors_ref, vectors_low_ref = refs
    arrived(0)
    arrived(1)
    centers_ref[...], centers_low_ref[...] = split_vectors(centroids_ref[...])
    valid = jnp.sum((ids_ref[...] >= 0).astype(jnp.float32), axis=1, keepdims=True)
    counts_ref[...] = jnp.broadcast_to(valid, counts_ref.shape).astype(jnp.int32)
    for k in range(stored_ref.shape[0]):
        arrived(2 + k)
        vectors_ref[k], vectors_low_ref[k] = split_vectors(stored_ref[k])


def copied_kernel(centroids_hbm, ids_hbm, stored_hbm, *refs):
    *outs, centroids_ref, ids_ref, stored_ref, sems = refs
    lists = stored_ref.shape[0]
    pairs = [(centroids_hbm, centroids_ref), (ids_hbm, ids_ref), *[(stored_hbm.at[k], stored_ref.at[k]) for k in range(lists)]]
    copies = copy_all(pairs, sems)
    split_lists(centroids_ref, ids_ref, stored_ref, *outs, arrived=lambda k: copies[k].wait())


def prepare(centroids, ids, stored, copied):
    lists, length, depth = stored.shape
    rows = lists * length + centroids.shape[0]
    scratch = [pltpu.VMEM(array.shape, array.dtype) for array in (centroids, ids, stored)]
    return pl.pallas_call(
        copied_kernel if copied else split_lists,
        out_shape=(
            jax.ShapeDtypeStruct(centroids.shape, jnp.bfloat16),
            jax.ShapeDtypeStruct(centroids.shape, EIGHT),
            jax.ShapeDtypeStruct((lists, TILE), jnp.int32),
            jax.ShapeDtypeStruct(stored.shape, jnp.bfloat16),
            jax.ShapeDtypeStruct(stored.shape, EIGHT),
        ),
        in_specs=[ANYWHERE if copied else WHOLE] * 3,
        out_specs=(WHOLE,) * 5,
        scratch_shapes=[*scratch, pltpu.SemaphoreType.DMA((2 + lists,))] if copied else [],
        compiler_params=pltpu.CompilerParams(vmem_limit_bytes=SMALL),
        cost_estimate=pl.CostEstimate(flops=6 * rows * depth, bytes_accessed=8 * rows * depth, transcendentals=0),
        name="prepare",
    )(centroids, ids, stored)


def score_kernel(blocks_ref, places_ref, *refs, rows_dev):
    *halves, out_ref, parts_ref, eighth_ref = refs
    devices = lax.axis_size("group") * lax.axis_size("member")
    odd = parity_of(here(), devices)
    chunks = TILE // rows_dev

    def place_of(chip):
        return jnp.where(odd == 1, position(chip, 1), position(chip, 0))

    first = place_of(here() >> 1)
    several = 32 // rows_dev
    for group in range(chunks // several):
        blocks = []
        for chunk in range(group * several, (group + 1) * several):
            offset = place_of(chunk if blocks_ref.shape[0] == TILE else pl.program_id(0) * chunks + chunk)
            source = pl.multiple_of((first ^ offset) * rows_dev, rows_dev)
            blocks.append(blocks_ref[pl.ds(source, rows_dev), :])
        queries = jnp.concatenate(blocks, axis=0)
        at = group * several * rows_dev
        high, low = split(queries)
        parts_ref[pl.ds(at, 32), :] = high
        parts_ref[pl.ds(TILE + at, 32), :] = low.astype(jnp.bfloat16)
        eighth_ref[pl.ds(at, 32), :] = queries.astype(EIGHT)

    def scores(vectors, vectors_low):
        terms = lax.dot_general(vectors[...], parts_ref[...], NT, preferred_element_type=jnp.float32)
        rest = lax.dot_general(vectors_low[...], eighth_ref[...], NT, preferred_element_type=jnp.float32)
        return terms[:, :TILE] + (terms[:, TILE:] + rest * (1 / SCALE))

    best = [jnp.full((1, TILE), LOWEST, jnp.float32) for _ in range(1 + places_ref.shape[0])]
    for side in range(2):
        centers_ref, centers_low_ref, counts_ref, vectors_ref, vectors_low_ref = halves[5 * side : 5 * side + 5]
        lists, length = vectors_ref.shape[:2]
        place = lax.broadcasted_iota(jnp.int32, (length, TILE), 0)
        for slot in range(lists):
            high, low = vectors_ref[slot], vectors_low_ref[slot]
            if side == 1 and slot == lists - 1:
                high = jnp.concatenate([high, halves[0][...], centers_ref[...]], axis=0)
                low = jnp.concatenate([low, halves[1][...], centers_low_ref[...]], axis=0)
            found = scores(high, low)
            if side == 1 and slot == lists - 1:
                best[0] = jnp.max(found[length:], axis=0, keepdims=True)
            usable = jnp.where(place < counts_ref[pl.ds(slot, 1), :], found[:length], LOWEST)
            found = jnp.max(usable, axis=0, keepdims=True)
            for step in range(places_ref.shape[0]):
                chosen = jnp.where(places_ref[pl.ds(step, 1), :] == slot, found, LOWEST)
                best[1 + step] = jnp.maximum(best[1 + step], chosen)
    best = [pltpu.roll(row, kind * rows_dev, 1) if kind else row for kind, row in enumerate(best)]
    lane_chip = lax.broadcasted_iota(jnp.int32, (1, TILE), 1) // rows_dev
    nothing = jnp.full((1, TILE), LOWEST, jnp.float32)
    for chip in range(chunks):
        row = best[0]
        for kind in range(1, len(best)):
            row = jnp.where(lane_chip == (chip + kind) % chunks, best[kind], row)
        straight = odd == parity_of(pl.program_id(0), devices) ^ parity(chip)
        out_ref[2 * chip] = jnp.where(straight, row, nothing)
        out_ref[2 * chip + 1] = jnp.where(straight, nothing, row)


def score(rows_dev, blocks, places, *halves):
    half, depth = blocks.shape
    kinds = 1 + places.shape[0]
    rows = 2 * (halves[0].shape[0] + halves[3].shape[0] * halves[3].shape[1])
    devices = 2 * TILE // rows_dev
    return pl.pallas_call(
        functools.partial(score_kernel, rows_dev=rows_dev),
        out_shape=jax.ShapeDtypeStruct((half // TILE * devices, 1, TILE), jnp.float32),
        grid=(half // TILE,),
        in_specs=[WHOLE, pl.BlockSpec((kinds - 1, TILE), lambda i: (0, i)), *[WHOLE] * len(halves)],
        out_specs=pl.BlockSpec((devices, 1, TILE), lambda i: (i, 0, 0)),
        scratch_shapes=[
            pltpu.VMEM((2 * TILE, depth), jnp.bfloat16),
            pltpu.VMEM((TILE, depth), EIGHT),
        ],
        compiler_params=pltpu.CompilerParams(vmem_limit_bytes=LARGE),
        cost_estimate=pl.CostEstimate(flops=8 * rows * half * depth, bytes_accessed=4 * rows * depth, transcendentals=0),
        name="score",
    )(blocks, places, *halves)


def finish_kernel(arrived_ref, coarse_ref, fine_ref, *, rows_dev):
    best = jnp.max(arrived_ref[...], axis=0)
    lane = ((here() >> 1) * rows_dev) % TILE
    best = pltpu.roll(best, (TILE - lane) % TILE, 1)
    coarse_ref[...] = best[0, :rows_dev]
    for step in range(fine_ref.shape[0]):
        fine_ref[pl.ds(step, 1), :] = best[:, (1 + step) * rows_dev : (2 + step) * rows_dev]


def finish(rows_dev, steps, arrived):
    return pl.pallas_call(
        functools.partial(finish_kernel, rows_dev=rows_dev),
        out_shape=(
            jax.ShapeDtypeStruct((rows_dev,), jnp.float32),
            jax.ShapeDtypeStruct((steps, rows_dev), jnp.float32),
        ),
        in_specs=[WHOLE],
        out_specs=(WHOLE, WHOLE),
        compiler_params=pltpu.CompilerParams(vmem_limit_bytes=SMALL),
        name="finish",
    )(arrived)


def gathered(blocks, stage):
    return [exchanged(blocks, masks) for masks in stage]


def in_hbm(*arrays):
    return [pltpu.with_memory_space_constraint(array, pltpu.HBM) for array in arrays]


def local(queries, centroids, stored, vector_ids, list_home, probes):
    devices = lax.axis_size("group") * lax.axis_size("member")
    rows_dev, lists = queries.shape[0], stored.shape[0]
    first, *rest = stages()
    arrived = gathered(queries, first)
    mine = (centroids, vector_ids, stored)
    theirs = [exchanged(array, (1, 1)) for array in mine]
    places, copied = lookup(devices // 2 * rows_dev, lists, *in_hbm(list_home, probes.transpose(1, 0, 2), queries))
    blocks = jnp.concatenate([copied, *arrived], axis=0)
    for number, stage in enumerate(rest):
        if number == len(rest) - 1:
            blocks, places, *mine = lax.optimization_barrier((blocks, places, *mine))
        arrived = gathered(blocks, stage)
        if number == len(rest) - 1:
            ready = prepare(*in_hbm(*mine), True), prepare(*theirs, False)
            arrived, ready = lax.optimization_barrier((arrived, ready))
        blocks = jnp.concatenate([blocks, *arrived], axis=0)
    parts = score(rows_dev, blocks, places, *ready[0], *ready[1])
    return finish(rows_dev, probes.shape[1], lax.all_to_all(parts, BOTH, 0, 0, tiled=True))


def solution(mesh):
    placed = (
        P(BOTH, None),
        P(BOTH, None),
        P("group", "member", None),
        P("group", "member"),
        P(),
        P(),
    )
    return jax.shard_map(
        local,
        mesh=mesh,
        in_specs=placed,
        out_specs=(P(BOTH), P(None, BOTH)),
        check_vma=False,
    )
```
